32 devices in a mesh: seg: 4 (over y, x), sub: 8 (over z, core).
Axes of the slice: x: 2, y: 2, z: 4, core: 2. Of those that a mesh axis runs over, the one named last changes fastest.
Arguments:
- diffusivity: float32 [256, 4096], P('seg', 'sub'), may hold values from 0.01 to 0.4
- background_flow: float32 [256, 4096], P('seg', 'sub'), may hold values from 0.5 to 2
- inlet_modes: float32 [512, 4096], P(None, 'sub'), may hold values from -0.25 to 0.25
- profile_step: float32 [512], P('sub'), may hold values from -6 to 6
- brick_owner: int32 [8192, 1], P(('seg', 'sub')), may hold values from 0 to 7; in each aligned block of 256 rows (0 to 255, 256 to 511, ...) at most 64 rows name the same one
- voxel_row: int32 [8192], P(('seg', 'sub')), may hold values from 0 to 15
- noise_weight: float32 [512, 128], P(('seg', 'sub')), may hold values from 0.1 to 10
- spread_matrix: float32 [128, 128], replicated, may hold values from -0.5 to 0.5
Outputs:
- forward_field: float32 [256, 4096], P('seg', 'sub')
- response: float32 [512, 128], P(('seg', 'sub'))
- product: float32 [512], P(('seg', 'sub'))
The draws below stay inside these ranges and needn't reach their ends.
Inputs may be any that keep to these rules, and one draw needn't show every extreme that they name: `brick_owner`: among the 256 blocks of one device each brick index is named at most 64 times, and exactly 64 times on some device; blocks go to bricks of their own segment group.
All inputs are finite; a program needn't handle non-finite values.
Results may differ from the reference program's by a relative error of at most 0.00019.
Values sent between devices are 32-bit elements; how exact they have to be, the bound alone decides.
A program may use at most 128 MiB of HBM per device.

```python
import math
import jax
import jax.numpy as jnp
import numpy as np
from jax import lax

AX = 64
CW = 512
BL = 128
VROWS = 16
NP = 512
NV = 2
SC = 2
NA = 256
NC = 4096
NB = 256
CAP = 64
BLOCKS = 8192
VOXROWS = 512
N_SEG = 4
N_SUB = 8


def set_ends(entries, own_key, smallest, high):
    longest = entries.shape.index(max(entries.shape))
    spots = []
    for shift in (0, 1):
        where = [jax.random.randint(jax.random.fold_in(own_key, axis), (), 0, length) for axis, length in enumerate(entries.shape)]
        where[longest] = (where[longest] + shift) % entries.shape[longest]
        spots.append(tuple(where))
    return entries.at[spots[0]].set(smallest).at[spots[1]].set(high)


def block_levels(key, shape, cuts, least, top_value):
    factor_of = 1.0
    for axis_at, parts in cuts:
        steps = jax.random.uniform(jax.random.fold_in(jax.random.fold_in(key, 6), axis_at), (parts,), jnp.float32, least / len(cuts), top_value / len(cuts))
        factor_of = factor_of * jnp.repeat(jnp.exp(steps), shape[axis_at] // parts).reshape((-1,) + (1,) * (len(shape) - 1 - axis_at))
    return factor_of


def routed_block(rng, own, number, rows, amount, top, limit, slope):
    ranking = jax.random.permutation(rng, amount)
    crowded, ordinary = shares(amount, rows * top, limit, slope, True), shares(amount, rows * top, limit, slope, False)
    places = jnp.arange(amount)

    def named(tallies, turn):
        used = int((tallies > 0).sum())
        fixed = max(1, used // 4)
        moved = fixed + (places - fixed + turn * (used - fixed)) % max(1, amount - fixed)
        return jnp.zeros((amount,), jnp.int32).at[ranking[jnp.where(places < fixed, places, moved)]].set(jnp.asarray(tallies, jnp.int32))

    tallies = jnp.where(number % 4 == 0, named(crowded, number // 4), named(ordinary, number - number // 4 - 1))
    mixed = jax.random.permutation(jax.random.fold_in(own, 3), amount)
    giver, sink = mixed[0:amount // 2 * 2:2], mixed[1:amount // 2 * 2:2]
    slack = jnp.minimum(tallies[giver] - 1, limit - tallies[sink]) // 2
    slack = jnp.where((giver == ranking[0]) | (sink == ranking[0]) | (tallies[sink] == 0), 0, jnp.maximum(slack, 0))
    moved = jax.random.randint(jax.random.fold_in(own, 4), (amount // 2,), 0, 1 << 20) % (slack + 1)
    tallies = tallies.at[giver].add(-moved).at[sink].add(moved)
    labels = jnp.searchsorted(jnp.cumsum(tallies), jnp.arange(rows * top), side="right").astype(jnp.int32)
    grid = labels.reshape(top, rows).T
    grid = grid[jax.random.permutation(jax.random.fold_in(own, 1), rows)]
    turn = jax.random.randint(jax.random.fold_in(own, 2), (rows, 1), 0, top)
    return jnp.take_along_axis(grid, (jnp.arange(top)[None, :] + turn) % top, axis=1)


def shares(amount, total, bound, slope, full):
    weights = [(1 << 20) // math.isqrt(grade ** slope) + 1 for grade in range(1, amount + 1)]
    largest = bound if full else min(bound, max(-(-total // amount), total * weights[0] // sum(weights)))
    least = 1 if total - largest >= amount - 1 else 0
    holding, surplus = [largest] + [least] * (amount - 1), total - largest - least * (amount - 1)
    while surplus > 0:
        candidates = [i for i in range(1, amount) if holding[i] < largest] or [i for i in range(1, amount) if holding[i] < bound]
        pool, budget = sum([weights[i] for i in candidates]), surplus
        for i in candidates:
            extra = min(bound - holding[i], max(1, budget * weights[i] // pool), surplus)
            holding[i] = holding[i] + extra
            surplus = surplus - extra
    return np.array(holding)


def noise(rng, dims, width, reach, shards=(), held_as=jnp.bfloat16):
    drawn = width * jax.random.normal(rng, dims, jnp.float32)
    if shards:
        drawn = drawn * block_levels(rng, dims, shards, -0.22, 0.18)
    return jnp.clip(drawn, -reach, reach).astype(held_as)


def setup_inputs(seed: int = 0) -> dict:
    key_list = jax.random.split(jax.random.key(seed), 9)
    diffusivity = jnp.clip(jnp.exp(math.log(0.4) - 3.6888795 * jax.random.uniform(key_list[0], (NA, NC), jnp.float32) ** block_levels(key_list[0], (NA, NC), ((0, 4), (1, 8)), -0.2, 0.2)), 0.01, 0.4)
    background_flow = jnp.clip(jnp.exp(math.log(2.0) - 1.3862944 * jax.random.uniform(key_list[1], (NA, NC), jnp.float32) ** block_levels(key_list[1], (NA, NC), ((0, 4), (1, 8)), -0.2, 0.2)), 0.5, 2.0)
    inlet_modes = noise(key_list[2], (NP, NC), NP ** -0.5, 0.25, ((1, 8),), jnp.float32)
    profile_step = noise(key_list[3], (NP,), 1.0, 6.0, ((0, 8),), jnp.float32)
    brick_owner_keys = jax.random.split(jax.random.fold_in(key_list[4], 1), BLOCKS // NB)
    brick_owner_turns = jax.random.permutation(jax.random.fold_in(key_list[4], 3), BLOCKS // NB)
    brick_owner = jax.vmap(lambda own, number: routed_block(jax.random.fold_in(key_list[4], 2), own, number, NB, N_SUB, 1, CAP, 2))(brick_owner_keys, brick_owner_turns).reshape((BLOCKS, 1))
    voxel_row = set_ends(jax.random.randint(key_list[5], (BLOCKS,), 0, VROWS), jax.random.fold_in(key_list[5], 1), 0, VROWS - 1).astype(jnp.int32)
    noise_weight = jnp.clip(jnp.exp(math.log(10.0) - 4.6051702 * jax.random.uniform(key_list[6], (VOXROWS, BL), jnp.float32) ** block_levels(key_list[6], (VOXROWS, BL), ((0, 32),), -0.2, 0.2)), 0.1, 10.0)
    spread_matrix = noise(key_list[7], (BL, BL), BL ** -0.5, 0.5, (), jnp.float32)
    return {"diffusivity": diffusivity, "background_flow": background_flow, "inlet_modes": inlet_modes, "profile_step": profile_step, "brick_owner": brick_owner, "voxel_row": voxel_row, "noise_weight": noise_weight, "spread_matrix": spread_matrix}


SIGMA = 0.001
HIGH = lax.Precision.HIGHEST


def from_above(field):
    return jnp.pad(field, ((1, 0), (0, 0)))[:-1]


def from_below(field):
    return jnp.pad(field, ((0, 1), (0, 0)))[1:]


def from_left(field):
    return jnp.pad(field, ((0, 0), (1, 0)))[:, :-1]


def from_right(field):
    return jnp.pad(field, ((0, 0), (0, 1)))[:, 1:]


def make_stencil(diffusion, flow, reaction):
    return (4.0 * diffusion + flow + reaction, diffusion + flow, diffusion, diffusion, diffusion)


def transpose_stencil(stencil):
    diagonal, upstream, downstream, leftward, rightward = stencil
    return (diagonal, from_above(downstream), from_below(upstream), from_left(rightward), from_right(leftward))


def apply_operator(field, stencil):
    diagonal, upstream, downstream, leftward, rightward = stencil
    return (diagonal * field - upstream * from_above(field) - downstream * from_below(field)
            - leftward * from_left(field) - rightward * from_right(field))


def recurrence(gains, driving, reverse):
    def advance(carry, pieces):
        value = pieces[0] * carry + pieces[1]
        return value, value

    start_value = jnp.zeros(gains.shape[1], jnp.float32)
    _, values = lax.scan(advance, start_value, (gains, driving), reverse=reverse)
    return values


def relax(field, source, stencil, forward):
    diagonal, upstream, downstream, leftward, rightward = stencil
    lateral = leftward * from_left(field) + rightward * from_right(field)
    if forward:
        explicit = source + downstream * from_below(field) + lateral
        return recurrence(upstream / diagonal, explicit / diagonal, False)
    explicit = source + upstream * from_above(field) + lateral
    return recurrence(downstream / diagonal, explicit / diagonal, True)


def restrict(field):
    height, breadth = field.shape
    return field.reshape(height // 2, 2, breadth // 2, 2).sum(axis=(1, 3))


def aggregate(field):
    return restrict(field) * 0.25


def prolong(field):
    return jnp.repeat(jnp.repeat(field, 2, axis=0), 2, axis=1)


def vcycle(field, source, finest, coarse, forward):
    field = relax(field, source, finest, forward)
    coarse_source = restrict(source - apply_operator(field, finest))
    correction = jnp.zeros_like(coarse_source)
    for sweep_index in range(SC):
        correction = relax(correction, coarse_source, coarse, forward)
    field = field + prolong(correction)
    return relax(field, source, finest, forward)


def solve(source, finest, coarse, forward):
    field = jnp.zeros_like(source)
    for cycle_index in range(NV):
        field = vcycle(field, source, finest, coarse, forward)
    return field


def to_blocks(field):
    return field.reshape(N_SEG, AX, N_SUB, CW).transpose(0, 2, 1, 3).reshape(-1, BL)


def from_blocks(blocks):
    return blocks.reshape(N_SEG, N_SUB, AX, CW).transpose(0, 2, 1, 3).reshape(N_SEG * AX, N_SUB * CW)


def reference(diffusivity, background_flow, inlet_modes, profile_step, brick_owner, voxel_row, noise_weight, spread_matrix):
    finest = make_stencil(diffusivity, background_flow, SIGMA)
    coarse = make_stencil(aggregate(diffusivity), 2.0 * aggregate(background_flow), 4.0 * SIGMA)
    profile = jnp.dot(profile_step, inlet_modes, precision=HIGH)
    inflow = diffusivity[0] + background_flow[0]
    source = jnp.zeros_like(diffusivity).at[0].set(inflow * profile)
    forward_field = solve(source, finest, coarse, True)
    blocks = to_blocks(forward_field)
    segment = jnp.arange(blocks.shape[0], dtype=jnp.int32) // (N_SUB * NB)
    target = ((segment * N_SUB + brick_owner[:, 0]) * VROWS + voxel_row).astype(jnp.int32)
    voxels = jax.ops.segment_sum(blocks, target, num_segments=N_SEG * N_SUB * VROWS)
    response = jnp.dot(voxels, spread_matrix.T, precision=HIGH)
    weighted = jnp.dot(noise_weight * response, spread_matrix, precision=HIGH)
    driving = from_blocks(weighted[target])
    adjoint_field = solve(driving, transpose_stencil(finest), transpose_stencil(coarse), False)
    inlet_flux = inflow * adjoint_field[0]
    product = jnp.dot(inlet_modes, inlet_flux, precision=HIGH)
    return forward_field, response, product
```

```python
import functools

import jax
import jax.numpy as jnp
from jax import lax
from jax.experimental import pallas as pl
from jax.experimental.pallas import tpu as pltpu
from jax.sharding import PartitionSpec as P

NV = 2
SC = 2
SIGMA = 0.001
HIGH = lax.Precision.HIGHEST
MESH = pl.DeviceIdType.MESH
LANES = 128
HALF = LANES // 2
CHUNKS = 8
VMEM_BYTES = 48 * 1024 * 1024


def lane_shift(value, amount):
    width = value.shape[-1]
    return pltpu.roll(value, amount % width, axis=value.ndim - 1)


def chunk_shift(value, amount):
    return pltpu.roll(value, amount % value.shape[0], axis=0)


def chunk_index(shape):
    return lax.broadcasted_iota(jnp.int32, shape, 0)


def row_above(value):
    last = value[-1]
    moved = jnp.where(chunk_index(last.shape) > 0, chunk_shift(last, 1), 0.0)
    return jnp.concatenate([moved[None], value[:-1]], axis=0)


def row_below(value):
    first = value[0]
    keep = chunk_index(first.shape) < first.shape[0] - 1
    moved = jnp.where(keep, chunk_shift(first, -1), 0.0)
    return jnp.concatenate([value[1:], moved[None]], axis=0)


def add_columns(value):
    lane = lax.broadcasted_iota(jnp.int32, value.shape, value.ndim - 1)
    partner = jnp.where(lane % 2 == 0, lane_shift(value, -1), lane_shift(value, 1))
    return value + partner


def restrict(value):
    steps = value.shape[0]
    pairs = value.reshape((steps // 2, 2) + value.shape[1:])
    return add_columns(pairs[:, 0] + pairs[:, 1])


def make_plan(diffusion, flow, reaction, stride, forward, inside):
    inverse = 1.0 / (4.0 * diffusion + flow + reaction)
    if forward:
        ahead, gain = diffusion, (diffusion + flow) * inverse
        leftward, rightward = diffusion, diffusion
    else:
        ahead = row_above(diffusion)
        gain = row_below(diffusion + flow) * inverse
        leftward = lane_shift(diffusion, stride) * inside
        rightward = lane_shift(diffusion, -stride) * inside
    steps = gain.shape[0]
    order = range(steps) if forward else range(steps - 1, -1, -1)
    products, running = [None] * steps, None
    for step in order:
        running = gain[step] if running is None else running * gain[step]
        products[step] = running
    count = running.shape[0]
    chunk = chunk_index(running.shape)
    level, jumps, distance = running, [], 1
    while distance < count:
        if forward:
            keep, amount = chunk >= distance, distance
        else:
            keep, amount = chunk < count - distance, -distance
        level = jnp.where(keep, level, 0.0)
        jumps.append(level)
        level = level * chunk_shift(level, amount)
        distance *= 2
    return {
        "inverse": inverse,
        "ahead": ahead,
        "left": leftward,
        "right": rightward,
        "gain": gain,
        "products": jnp.stack(products),
        "jumps": jumps,
        "stride": stride,
        "forward": forward,
    }


def explicit_part(field, plan):
    stride = plan["stride"]
    beside = row_below(field) if plan["forward"] else row_above(field)
    return (
        plan["ahead"] * beside
        + plan["left"] * lane_shift(field, stride)
        + plan["right"] * lane_shift(field, -stride)
    )


def run_rows(driving, plan):
    forward, gain = plan["forward"], plan["gain"]
    steps, count = driving.shape[0], driving.shape[1]
    order = range(steps) if forward else range(steps - 1, -1, -1)
    local, running = [None] * steps, None
    for step in order:
        running = driving[step] if running is None else gain[step] * running + driving[step]
        local[step] = running
    total, distance = running, 1
    for jump in plan["jumps"]:
        total = total + jump * chunk_shift(total, distance if forward else -distance)
        distance *= 2
    chunk = chunk_index(total.shape)
    if forward:
        carry = jnp.where(chunk > 0, chunk_shift(total, 1), 0.0)
    else:
        carry = jnp.where(chunk < count - 1, chunk_shift(total, -1), 0.0)
    return jnp.stack(local) + plan["products"] * carry[None]


def solve(source, finest, coarse):
    field = None
    for cycle_index in range(NV):
        old = None if field is None else explicit_part(field, finest)
        total = source if old is None else source + old
        field = run_rows(total * finest["inverse"], finest)
        new = explicit_part(field, finest)
        coarse_source = restrict(new if old is None else new - old)
        correction = run_rows(coarse_source * coarse["inverse"], coarse)
        for sweep_index in range(1, SC):
            total = coarse_source + explicit_part(correction, coarse)
            correction = run_rows(total * coarse["inverse"], coarse)
        steps = field.shape[0]
        pairs = field.reshape((steps // 2, 2) + field.shape[1:]) + correction[:, None]
        field = pairs.reshape(field.shape)
        total = source + explicit_part(field, finest)
        field = run_rows(total * finest["inverse"], finest)
    return field


def plans(diffusion, flow, forward, inside):
    finest = make_plan(diffusion, flow, SIGMA, 1, forward, inside)
    coarse = make_plan(
        restrict(diffusion) * 0.25, restrict(flow) * 0.5, 4.0 * SIGMA, 2, forward, inside
    )
    return finest, coarse


def take_steps(ref, index):
    rows = ref.shape[-2]
    length = rows // CHUNKS
    halves = [
        jnp.stack([ref[index, half, pl.ds(step, CHUNKS, stride=length), :] for step in range(length)])
        for half in range(2)
    ]
    return jnp.concatenate(halves, axis=2)


def forward_kernel(strips_ref, profile_ref, field_ref):
    diffusion, flow = take_steps(strips_ref, 0), take_steps(strips_ref, 1)
    finest, coarse = plans(diffusion, flow, True, None)
    first = (diffusion[0] + flow[0]) * profile_ref[...]
    first = jnp.where(chunk_index(first.shape) == 0, first, 0.0)
    source = jnp.concatenate([first[None], jnp.zeros_like(diffusion[1:])], axis=0)
    field = solve(source, finest, coarse)
    length = field.shape[0]
    for step in range(length):
        field_ref[pl.ds(step, CHUNKS, stride=length), :] = field[step, :, :LANES]


def inside_mask(shape, strip, strips, group, groups):
    lane = lax.broadcasted_iota(jnp.int32, shape, len(shape) - 1)
    no_left = jnp.where((strip == 0) & (group == 0), 1, 0)
    no_right = jnp.where((strip == strips - 1) & (group == groups - 1), 1, 0)
    limit_high = jnp.where(no_left == 1, LANES + HALF, 2 * LANES)
    limit_low = jnp.where(no_right == 1, LANES, LANES + HALF)
    outside = (lane >= limit_high) | ((lane >= limit_low) & (lane < LANES + HALF))
    return jnp.where(outside, 0.0, 1.0)


def adjoint_kernel(seg, sub, strips_ref, driving_ref, modes_ref, partial_ref):
    strip, group = lax.axis_index("seg"), lax.axis_index("sub")
    diffusion, flow = take_steps(strips_ref, 0), take_steps(strips_ref, 1)
    inside = inside_mask((1, 1, 2 * LANES), strip, seg, group, sub)
    finest, coarse = plans(diffusion, flow, False, inside)
    field = solve(take_steps(driving_ref, 0), finest, coarse)
    flux = ((diffusion[0] + flow[0]) * field[0])[:, :LANES]
    flux = jnp.where(chunk_index(flux.shape) == 0, flux, 0.0)
    modes = modes_ref[:, pl.ds(pl.multiple_of(strip * LANES, LANES), LANES)]
    sums = lax.dot_general(
        flux, modes, (((1,), (1,)), ((), ())), precision=HIGH, preferred_element_type=jnp.float32
    )
    partial_ref[...] = sums


def enter(seg, sub, diagonal):
    strip, group = lax.axis_index("seg"), lax.axis_index("sub")
    barrier = pltpu.get_barrier_semaphore()

    def greet(to_strip, to_group):
        pl.semaphore_signal(barrier, inc=1, device_id=(to_strip, to_group), device_id_type=MESH)

    for k in range(1, seg):
        greet(lax.rem(strip + k, seg), group)
    for k in range(1, sub):
        greet(strip, lax.rem(group + k, sub))
    if diagonal:

        @pl.when(strip == 0)
        def _():
            for other in range(seg):
                greet(other, lax.rem(group + sub - 1, sub))

        @pl.when(strip == seg - 1)
        def _():
            for other in range(seg):
                greet(other, lax.rem(group + 1, sub))

    pl.semaphore_wait(barrier, seg - 1 + sub - 1 + (2 if diagonal else 0))


def remote(source, target, send, receive, to_strip, to_group):
    return pltpu.make_async_remote_copy(
        src_ref=source,
        dst_ref=target,
        send_sem=send,
        recv_sem=receive,
        device_id=(to_strip, to_group),
        device_id_type=MESH,
    )


def start_reshard(seg, sub, fields, packed, edges, strips_ref, edge_ref, sems):
    seg_send, seg_recv, edge_send, edge_recv = sems
    strip, group = lax.axis_index("seg"), lax.axis_index("sub")
    rows = packed.shape[3]
    lane = lax.broadcasted_iota(jnp.int32, (rows, LANES), 1)
    for index, field in enumerate(fields):
        edges[0, index] = field[:, (seg - 1) * LANES : seg * LANES]
        edges[1, index] = field[:, :LANES]
    here = pl.ds(pl.multiple_of(strip * rows, rows), rows)
    copies = [
        remote(edges.at[0], edge_ref.at[:, here, :], edge_send.at[0], edge_recv.at[strip],
               0, lax.rem(group + 1, sub)),
        remote(edges.at[1], edge_ref.at[:, here, :], edge_send.at[1], edge_recv.at[strip],
               seg - 1, lax.rem(group + sub - 1, sub)),
    ]
    for copy in copies:
        copy.start()
    for index, field in enumerate(fields):
        tiles = [field[:, t * LANES : (t + 1) * LANES] for t in range(seg)]
        for t in range(seg):
            packed[t, index, 0] = tiles[t]
            packed[t, index, 1] = jnp.where(
                lane < HALF, tiles[min(t + 1, seg - 1)], tiles[max(t - 1, 0)]
            )
    for k in range(1, seg):
        peer = lax.rem(strip + k, seg)
        copy = remote(packed.at[peer], strips_ref.at[:, :, here, :], seg_send.at[k], seg_recv.at[strip],
                      peer, group)
        copy.start()
        copies.append(copy)
    strips_ref[:, :, here, :] = packed[strip]
    return copies


def finish_reshard(seg, sub, copies, strips_ref, edge_ref, packed, sems):
    seg_send, seg_recv, edge_send, edge_recv = sems
    strip, group = lax.axis_index("seg"), lax.axis_index("sub")
    rows = packed.shape[3]
    for k in range(1, seg):
        peer = lax.rem(strip + k, seg)
        there = pl.ds(pl.multiple_of(peer * rows, rows), rows)
        remote(packed.at[peer], strips_ref.at[:, :, there, :], seg_send.at[k], seg_recv.at[peer],
               peer, group).wait_recv()

    def edge_arrivals():
        for other in range(seg):
            there = pl.ds(other * rows, rows)
            remote(packed.at[other, :, 0], edge_ref.at[:, there, :], edge_send.at[0],
                   edge_recv.at[other], 0, group).wait_recv()

    lane = lax.broadcasted_iota(jnp.int32, edge_ref.shape, 2)

    @pl.when(strip == 0)
    def _():
        edge_arrivals()
        known = jnp.where(group > 0, 1.0, 0.0)
        strips_ref[:, 1] = jnp.where(
            lane >= HALF, edge_ref[...] * known, strips_ref[:, 1]
        )

    @pl.when(strip == seg - 1)
    def _():
        edge_arrivals()
        known = jnp.where(group < sub - 1, 1.0, 0.0)
        strips_ref[:, 1] = jnp.where(
            lane < HALF, edge_ref[...] * known, strips_ref[:, 1]
        )

    for copy in copies:
        copy.wait_send()


def share(count, me, source_of, target_of, send, recv, place):
    started = []
    for k in range(1, count):
        peer = lax.rem(me + k, count)
        copy = remote(source_of(peer), target_of(me), send.at[k], recv.at[me], *place(peer))
        copy.start()
        started.append(copy)

    def arrive():
        for k in range(1, count):
            peer = lax.rem(me + count - k, count)
            remote(source_of(peer), target_of(peer), send.at[k], recv.at[peer],
                   *place(peer)).wait_recv()

    def left():
        for copy in started:
            copy.wait_send()

    return arrive, left


def intake_kernel(seg, sub, diffusivity_ref, flow_ref, modes_ref, step_ref, strips_ref, profile_ref,
                  packed, edges, edge_ref, steps, own, sides,
                  seg_send, seg_recv, edge_send, edge_recv, step_send, step_recv, side_send, side_recv):
    strip, group = lax.axis_index("seg"), lax.axis_index("sub")
    sems = (seg_send, seg_recv, edge_send, edge_recv)
    enter(seg, sub, True)
    arrive, left = share(
        sub, group, lambda peer: step_ref, lambda whose: steps.at[whose], step_send, step_recv,
        lambda peer: (strip, peer),
    )
    steps[group] = step_ref[...]
    copies = start_reshard(seg, sub, [diffusivity_ref[...], flow_ref[...]], packed, edges, strips_ref,
                           edge_ref, sems)
    arrive()
    depth = modes_ref.shape[0] // sub
    columns = steps[...].reshape(sub, LANES)
    total = None
    turned = columns.T
    for whose in range(sub):
        weight = turned[:depth, whose : whose + 1]
        term = weight * modes_ref[whose * depth : (whose + 1) * depth, :]
        total = term if total is None else total + term
    profile = jnp.sum(total, axis=0, keepdims=True)
    for t in range(seg):
        own[t + 1] = profile[:, t * LANES : (t + 1) * LANES]
    right = remote(own.at[seg], sides.at[0], side_send.at[0], side_recv.at[0],
                   strip, lax.rem(group + 1, sub))
    back = remote(own.at[1], sides.at[1], side_send.at[1], side_recv.at[1],
                  strip, lax.rem(group + sub - 1, sub))
    right.start()
    back.start()
    finish_reshard(seg, sub, copies, strips_ref, edge_ref, packed, sems)
    right.wait()
    back.wait()
    own[0] = sides[0]
    own[seg + 1] = sides[1]
    lane = lax.broadcasted_iota(jnp.int32, (1, LANES), 1)
    profile_ref[:, :LANES] = own[strip + 1]
    profile_ref[:, LANES:] = jnp.where(lane < HALF, own[strip + 2], own[strip])
    left()


def voxel_kernel(seg, sub, field_ref, target_row_ref, target_column_ref, noise_ref, spread_ref,
                 forward_ref, response_ref, driving_ref,
                 blocks, partial, arrived, weighted, gathered, packed, edges, edge_ref,
                 block_send, block_recv, sum_send, sum_recv, row_send, row_recv,
                 seg_send, seg_recv, edge_send, edge_recv):
    strip, group = lax.axis_index("seg"), lax.axis_index("sub")
    sems = (seg_send, seg_recv, edge_send, edge_recv)
    rows = blocks.shape[1]
    voxel_rows = noise_ref.shape[0]
    enter(seg, sub, True)

    def rows_of(whose):
        return pl.ds(pl.multiple_of(whose * rows, rows), rows)

    def voxels_of(whose):
        return pl.ds(pl.multiple_of(whose * voxel_rows, voxel_rows), voxel_rows)

    arrive, left_blocks = share(
        seg, strip, lambda peer: field_ref.at[rows_of(peer), :], lambda whose: blocks.at[whose],
        block_send, block_recv, lambda peer: (peer, group),
    )
    blocks[strip] = field_ref[rows_of(strip), :]
    arrive()
    total = None
    for t in range(seg):
        block = blocks[t]
        forward_ref[:, t * LANES : (t + 1) * LANES] = block
        voxel = lax.broadcasted_iota(jnp.int32, (sub * voxel_rows, rows), 0)
        chosen = jnp.where(voxel == target_row_ref[t : t + 1, :], 1.0, 0.0)
        term = jnp.dot(chosen, block, precision=HIGH, preferred_element_type=jnp.float32)
        total = term if total is None else total + term
    partial[...] = total
    arrive, left_sums = share(
        sub, group, lambda peer: partial.at[voxels_of(peer), :], lambda whose: arrived.at[whose],
        sum_send, sum_recv, lambda peer: (strip, peer),
    )
    arrived[group] = partial[voxels_of(group), :]
    arrive()
    voxels = arrived[0]
    for whose in range(1, sub):
        voxels = voxels + arrived[whose]
    spread = spread_ref[...]
    response = lax.dot_general(
        voxels, spread, (((1,), (1,)), ((), ())), precision=HIGH, preferred_element_type=jnp.float32
    )
    response_ref[...] = response
    weighted[...] = jnp.dot(
        noise_ref[...] * response, spread, precision=HIGH, preferred_element_type=jnp.float32
    )
    arrive, left_rows = share(
        sub, group, lambda peer: weighted, lambda whose: gathered.at[voxels_of(whose), :],
        row_send, row_recv, lambda peer: (strip, peer),
    )
    gathered[voxels_of(group), :] = weighted[...]
    arrive()
    everything = gathered[...]
    tiles = []
    for t in range(seg):
        voxel = lax.broadcasted_iota(jnp.int32, (rows, sub * voxel_rows), 1)
        chosen = jnp.where(voxel == target_column_ref[:, t : t + 1], 1.0, 0.0)
        tiles.append(jnp.dot(chosen, everything, precision=HIGH, preferred_element_type=jnp.float32))
    copies = start_reshard(seg, sub, [jnp.concatenate(tiles, axis=1)], packed, edges, driving_ref,
                           edge_ref, sems)
    finish_reshard(seg, sub, copies, driving_ref, edge_ref, packed, sems)
    left_blocks()
    left_sums()
    left_rows()


def product_kernel(seg, sub, partial_ref, product_ref, mine, arrived, second, total,
                   sub_send, sub_recv, seg_send, seg_recv):
    strip, group = lax.axis_index("seg"), lax.axis_index("sub")
    enter(seg, sub, False)
    mine[...] = partial_ref[0:1, :]
    arrive, left_first = share(
        sub, group, lambda peer: mine, lambda whose: arrived.at[whose], sub_send, sub_recv,
        lambda peer: (strip, peer),
    )
    arrived[group] = mine[...]
    arrive()
    value = arrived[0]
    for whose in range(1, sub):
        value = value + arrived[whose]
    total[...] = value
    arrive, left_second = share(
        seg, strip, lambda peer: total, lambda whose: second.at[whose], seg_send, seg_recv,
        lambda peer: (peer, group),
    )
    second[strip] = value
    arrive()
    value = second[0]
    for whose in range(1, seg):
        value = value + second[whose]
    product_ref[...] = value
    left_first()
    left_second()


def on_device(seg, sub, diffusivity, background_flow, inlet_modes, profile_step, brick_owner,
              voxel_row, noise_weight, spread_matrix):
    vmem = pl.BlockSpec(memory_space=pltpu.VMEM)
    f32 = jnp.float32
    rows, width = diffusivity.shape
    modes = inlet_modes.shape[0]
    voxel_rows = noise_weight.shape[0]
    total_rows = rows * seg
    dma = pltpu.SemaphoreType.DMA

    def call(kernel, shapes, scratch, collective):
        return pl.pallas_call(
            kernel,
            out_shape=[jax.ShapeDtypeStruct(shape, f32) for shape in shapes],
            out_specs=[vmem] * len(shapes),
            scratch_shapes=scratch,
            compiler_params=pltpu.CompilerParams(
                vmem_limit_bytes=VMEM_BYTES,
                **({} if collective is None else {"collective_id": collective, "has_side_effects": True}),
            ),
        )

    reshard_sems = [dma((seg,)), dma((seg,)), dma((2,)), dma((seg,))]
    step_row = jnp.pad(profile_step[None, :], ((0, 0), (0, LANES - profile_step.shape[0])))
    strips, profile = call(
        functools.partial(intake_kernel, seg, sub),
        [(2, 2, total_rows, LANES), (1, 2 * LANES)],
        [
            pltpu.VMEM((seg, 2, 2, rows, LANES), f32),
            pltpu.VMEM((2, 2, rows, LANES), f32),
            pltpu.VMEM((2, total_rows, LANES), f32),
            pltpu.VMEM((sub, 1, LANES), f32),
            pltpu.VMEM((seg + 2, 1, LANES), f32),
            pltpu.VMEM((2, 1, LANES), f32),
            *reshard_sems,
            dma((sub,)), dma((sub,)), dma((2,)), dma((2,)),
        ],
        0,
    )(diffusivity, background_flow, inlet_modes, step_row)
    (strip_field,) = call(forward_kernel, [(total_rows, LANES)], [], None)(strips, profile)
    target = (brick_owner[:, 0] * voxel_rows + voxel_row).reshape(rows, seg)
    forward_field, response, driving = call(
        functools.partial(voxel_kernel, seg, sub),
        [(rows, width), (voxel_rows, LANES), (1, 2, total_rows, LANES)],
        [
            pltpu.VMEM((seg, rows, LANES), f32),
            pltpu.VMEM((sub * voxel_rows, LANES), f32),
            pltpu.VMEM((sub, voxel_rows, LANES), f32),
            pltpu.VMEM((voxel_rows, LANES), f32),
            pltpu.VMEM((sub * voxel_rows, LANES), f32),
            pltpu.VMEM((seg, 1, 2, rows, LANES), f32),
            pltpu.VMEM((2, 1, rows, LANES), f32),
            pltpu.VMEM((1, total_rows, LANES), f32),
            dma((seg,)), dma((seg,)), dma((sub,)), dma((sub,)), dma((sub,)), dma((sub,)),
            *reshard_sems,
        ],
        1,
    )(strip_field, target.T, target, noise_weight, spread_matrix)
    (partial,) = call(functools.partial(adjoint_kernel, seg, sub), [(CHUNKS, modes)], [], None)(
        strips, driving, inlet_modes
    )
    (product,) = call(
        functools.partial(product_kernel, seg, sub),
        [(1, modes)],
        [
            pltpu.VMEM((1, modes), f32),
            pltpu.VMEM((sub, 1, modes), f32),
            pltpu.VMEM((seg, 1, modes), f32),
            pltpu.VMEM((1, modes), f32),
            dma((sub,)), dma((sub,)), dma((seg,)), dma((seg,)),
        ],
        2,
    )(partial)
    share_of = modes // (seg * sub)
    place = lax.axis_index("seg") * sub + lax.axis_index("sub")
    return (forward_field, response, lax.dynamic_slice(product[0], (place * share_of,), (share_of,)))


def solution(mesh):
    return jax.shard_map(
        functools.partial(on_device, mesh.shape["seg"], mesh.shape["sub"]),
        mesh=mesh,
        in_specs=(
            P("seg", "sub"),
            P("seg", "sub"),
            P(None, "sub"),
            P("sub"),
            P(("seg", "sub"), None),
            P(("seg", "sub")),
            P(("seg", "sub"), None),
            P(),
        ),
        out_specs=(P("seg", "sub"), P(("seg", "sub"), None), P(("seg", "sub"))),
        check_vma=False,
    )
```

```python
import functools

import jax
import jax.numpy as jnp
from jax import lax
from jax.experimental import pallas as pl
from jax.experimental.pallas import tpu as pltpu
from jax.sharding import PartitionSpec as P

NV = 2
SC = 2
SIGMA = 0.001
HIGH = lax.Precision.HIGHEST
MESH = pl.DeviceIdType.MESH
LANES = 128
HALF = LANES // 2
CHUNKS = 8
VMEM_BYTES = 48 * 1024 * 1024


def lane_shift(value, amount):
    width = value.shape[-1]
    return pltpu.roll(value, amount % width, axis=value.ndim - 1)


def chunk_shift(value, amount):
    return pltpu.roll(value, amount % value.shape[0], axis=0)


def chunk_index(shape):
    return lax.broadcasted_iota(jnp.int32, shape, 0)


def row_above(value):
    last = value[-1]
    moved = jnp.where(chunk_index(last.shape) > 0, chunk_shift(last, 1), 0.0)
    return jnp.concatenate([moved[None], value[:-1]], axis=0)


def row_below(value):
    first = value[0]
    keep = chunk_index(first.shape) < first.shape[0] - 1
    moved = jnp.where(keep, chunk_shift(first, -1), 0.0)
    return jnp.concatenate([value[1:], moved[None]], axis=0)


def add_columns(value):
    lane = lax.broadcasted_iota(jnp.int32, value.shape, value.ndim - 1)
    partner = jnp.where(lane % 2 == 0, lane_shift(value, -1), lane_shift(value, 1))
    return value + partner


def restrict(value):
    steps = value.shape[0]
    pairs = value.reshape((steps // 2, 2) + value.shape[1:])
    return add_columns(pairs[:, 0] + pairs[:, 1])


def make_plan(diffusion, flow, reaction, stride, forward, inside):
    inverse = 1.0 / (4.0 * diffusion + flow + reaction)
    if forward:
        ahead, gain = diffusion, (diffusion + flow) * inverse
        leftward, rightward = diffusion, diffusion
    else:
        ahead = row_above(diffusion)
        gain = row_below(diffusion + flow) * inverse
        leftward = lane_shift(diffusion, stride) * inside
        rightward = lane_shift(diffusion, -stride) * inside
    steps = gain.shape[0]
    order = range(steps) if forward else range(steps - 1, -1, -1)
    products, running = [None] * steps, None
    for step in order:
        running = gain[step] if running is None else running * gain[step]
        products[step] = running
    count = running.shape[0]
    chunk = chunk_index(running.shape)
    level, jumps, distance = running, [], 1
    while distance < count:
        if forward:
            keep, amount = chunk >= distance, distance
        else:
            keep, amount = chunk < count - distance, -distance
        level = jnp.where(keep, level, 0.0)
        jumps.append(level)
        level = level * chunk_shift(level, amount)
        distance *= 2
    return {
        "inverse": inverse,
        "ahead": ahead,
        "left": leftward,
        "right": rightward,
        "gain": gain,
        "products": jnp.stack(products),
        "jumps": jumps,
        "stride": stride,
        "forward": forward,
    }


def explicit_part(field, plan):
    stride = plan["stride"]
    beside = row_below(field) if plan["forward"] else row_above(field)
    return (
        plan["ahead"] * beside
        + plan["left"] * lane_shift(field, stride)
        + plan["right"] * lane_shift(field, -stride)
    )


def run_rows(driving, plan):
    forward, gain = plan["forward"], plan["gain"]
    steps, count = driving.shape[0], driving.shape[1]
    order = range(steps) if forward else range(steps - 1, -1, -1)
    local, running = [None] * steps, None
    for step in order:
        running = driving[step] if running is None else gain[step] * running + driving[step]
        local[step] = running
    total, distance = running, 1
    for jump in plan["jumps"]:
        total = total + jump * chunk_shift(total, distance if forward else -distance)
        distance *= 2
    chunk = chunk_index(total.shape)
    if forward:
        carry = jnp.where(chunk > 0, chunk_shift(total, 1), 0.0)
    else:
        carry = jnp.where(chunk < count - 1, chunk_shift(total, -1), 0.0)
    return jnp.stack(local) + plan["products"] * carry[None]


def solve(source, finest, coarse):
    field = None
    for cycle_index in range(NV):
        old = None if field is None else explicit_part(field, finest)
        total = source if old is None else source + old
        field = run_rows(total * finest["inverse"], finest)
        new = explicit_part(field, finest)
        coarse_source = restrict(new if old is None else new - old)
        correction = run_rows(coarse_source * coarse["inverse"], coarse)
        for sweep_index in range(1, SC):
            total = coarse_source + explicit_part(correction, coarse)
            correction = run_rows(total * coarse["inverse"], coarse)
        steps = field.shape[0]
        pairs = field.reshape((steps // 2, 2) + field.shape[1:]) + correction[:, None]
        field = pairs.reshape(field.shape)
        total = source + explicit_part(field, finest)
        field = run_rows(total * finest["inverse"], finest)
    return field


def plans(diffusion, flow, forward, inside):
    finest = make_plan(diffusion, flow, SIGMA, 1, forward, inside)
    coarse = make_plan(
        restrict(diffusion) * 0.25, restrict(flow) * 0.5, 4.0 * SIGMA, 2, forward, inside
    )
    return finest, coarse


def take_steps(ref, index):
    rows = ref.shape[-2]
    length = rows // CHUNKS
    halves = [
        jnp.stack([ref[index, half, pl.ds(step, CHUNKS, stride=length), :] for step in range(length)])
        for half in range(2)
    ]
    return jnp.concatenate(halves, axis=2)


def forward_step(strips_ref, profile_ref, field_ref):
    diffusion, flow = take_steps(strips_ref, 0), take_steps(strips_ref, 1)
    finest, coarse = plans(diffusion, flow, True, None)
    first = (diffusion[0] + flow[0]) * profile_ref[...]
    first = jnp.where(chunk_index(first.shape) == 0, first, 0.0)
    source = jnp.concatenate([first[None], jnp.zeros_like(diffusion[1:])], axis=0)
    field = solve(source, finest, coarse)
    length = field.shape[0]
    for step in range(length):
        field_ref[pl.ds(step, CHUNKS, stride=length), :] = field[step, :, :LANES]


def inside_mask(shape, strip, strips, group, groups):
    lane = lax.broadcasted_iota(jnp.int32, shape, len(shape) - 1)
    no_left = jnp.where((strip == 0) & (group == 0), 1, 0)
    no_right = jnp.where((strip == strips - 1) & (group == groups - 1), 1, 0)
    limit_high = jnp.where(no_left == 1, LANES + HALF, 2 * LANES)
    limit_low = jnp.where(no_right == 1, LANES, LANES + HALF)
    outside = (lane >= limit_high) | ((lane >= limit_low) & (lane < LANES + HALF))
    return jnp.where(outside, 0.0, 1.0)


def adjoint_step(seg, sub, strips_ref, driving_ref, modes_ref, partial_ref):
    strip, group = lax.axis_index("seg"), lax.axis_index("sub")
    diffusion, flow = take_steps(strips_ref, 0), take_steps(strips_ref, 1)
    inside = inside_mask((1, 1, 2 * LANES), strip, seg, group, sub)
    finest, coarse = plans(diffusion, flow, False, inside)
    field = solve(take_steps(driving_ref, 0), finest, coarse)
    flux = ((diffusion[0] + flow[0]) * field[0])[:, :LANES]
    flux = jnp.where(chunk_index(flux.shape) == 0, flux, 0.0)
    modes = modes_ref[:, pl.ds(pl.multiple_of(strip * LANES, LANES), LANES)]
    sums = lax.dot_general(
        flux, modes, (((1,), (1,)), ((), ())), precision=HIGH, preferred_element_type=jnp.float32
    )
    partial_ref[...] = sums


def enter(seg, sub):
    count = seg * sub
    me = lax.axis_index("seg") * sub + lax.axis_index("sub")
    barrier = pltpu.get_barrier_semaphore()
    for k in range(1, count):
        peer = lax.rem(me + k, count)
        pl.semaphore_signal(
            barrier, inc=1, device_id=(peer // sub, lax.rem(peer, sub)), device_id_type=MESH
        )
    pl.semaphore_wait(barrier, count - 1)


def remote(source, target, send, receive, to_strip, to_group):
    return pltpu.make_async_remote_copy(
        src_ref=source,
        dst_ref=target,
        send_sem=send,
        recv_sem=receive,
        device_id=(to_strip, to_group),
        device_id_type=MESH,
    )


def start_reshard(seg, sub, fields, packed, edges, strips_ref, edge_ref, sems):
    seg_send, seg_recv, edge_send, edge_recv = sems
    strip, group = lax.axis_index("seg"), lax.axis_index("sub")
    rows = packed.shape[3]
    lane = lax.broadcasted_iota(jnp.int32, (rows, LANES), 1)
    for index, field in enumerate(fields):
        edges[0, index] = field[:, (seg - 1) * LANES : seg * LANES]
        edges[1, index] = field[:, :LANES]
    here = pl.ds(pl.multiple_of(strip * rows, rows), rows)
    copies = [
        remote(edges.at[0], edge_ref.at[:, here, :], edge_send.at[0], edge_recv.at[strip],
               0, lax.rem(group + 1, sub)),
        remote(edges.at[1], edge_ref.at[:, here, :], edge_send.at[1], edge_recv.at[strip],
               seg - 1, lax.rem(group + sub - 1, sub)),
    ]
    for copy in copies:
        copy.start()
    for index, field in enumerate(fields):
        tiles = [field[:, t * LANES : (t + 1) * LANES] for t in range(seg)]
        for t in range(seg):
            packed[t, index, 0] = tiles[t]
            packed[t, index, 1] = jnp.where(
                lane < HALF, tiles[min(t + 1, seg - 1)], tiles[max(t - 1, 0)]
            )
    for k in range(1, seg):
        peer = lax.rem(strip + k, seg)
        copy = remote(packed.at[peer], strips_ref.at[:, :, here, :], seg_send.at[k], seg_recv.at[strip],
                      peer, group)
        copy.start()
        copies.append(copy)
    strips_ref[:, :, here, :] = packed[strip]
    return copies


def finish_reshard(seg, sub, copies, strips_ref, edge_ref, packed, sems):
    seg_send, seg_recv, edge_send, edge_recv = sems
    strip, group = lax.axis_index("seg"), lax.axis_index("sub")
    rows = packed.shape[3]
    for k in range(1, seg):
        peer = lax.rem(strip + k, seg)
        there = pl.ds(pl.multiple_of(peer * rows, rows), rows)
        remote(packed.at[peer], strips_ref.at[:, :, there, :], seg_send.at[k], seg_recv.at[peer],
               peer, group).wait_recv()

    def edge_arrivals():
        for other in range(seg):
            there = pl.ds(other * rows, rows)
            remote(packed.at[other, :, 0], edge_ref.at[:, there, :], edge_send.at[0],
                   edge_recv.at[other], 0, group).wait_recv()

    lane = lax.broadcasted_iota(jnp.int32, edge_ref.shape, 2)

    @pl.when(strip == 0)
    def _():
        edge_arrivals()
        known = jnp.where(group > 0, 1.0, 0.0)
        strips_ref[:, 1] = jnp.where(
            lane >= HALF, edge_ref[...] * known, strips_ref[:, 1]
        )

    @pl.when(strip == seg - 1)
    def _():
        edge_arrivals()
        known = jnp.where(group < sub - 1, 1.0, 0.0)
        strips_ref[:, 1] = jnp.where(
            lane < HALF, edge_ref[...] * known, strips_ref[:, 1]
        )

    for copy in copies:
        copy.wait_send()


def share(count, me, source_of, target_of, send, recv, place):
    started = []
    for k in range(1, count):
        peer = lax.rem(me + k, count)
        copy = remote(source_of(peer), target_of(me), send.at[k], recv.at[me], *place(peer))
        copy.start()
        started.append(copy)

    def arrive():
        for k in range(1, count):
            peer = lax.rem(me + count - k, count)
            remote(source_of(peer), target_of(peer), send.at[k], recv.at[peer],
                   *place(peer)).wait_recv()

    def left():
        for copy in started:
            copy.wait_send()

    return arrive, left


def choose(chosen, values):
    high = values.astype(jnp.bfloat16)
    rest = values - high.astype(jnp.float32)
    middle = rest.astype(jnp.bfloat16)
    low = (rest - middle.astype(jnp.float32)).astype(jnp.bfloat16)
    picks = chosen.astype(jnp.bfloat16)
    parts = [jnp.dot(picks, part, preferred_element_type=jnp.float32) for part in (low, middle, high)]
    return parts[0] + parts[1] + parts[2]


def whole_kernel(seg, sub, diffusivity_hbm, flow_hbm, modes_hbm, step_ref, target_row_ref,
                 target_column_ref, noise_ref, spread_ref,
                 forward_ref, response_ref, product_ref,
                 diffusivity, flow, modes, strips, profile, field, driving, partial_product,
                 packed, edges, edge_in, packed_one, edges_one, edge_in_one,
                 steps, own, sides, targets, partial, arrived, weighted, gathered, blocks, mine, products,
                 load_sem, step_send, step_recv, side_send, side_recv, target_send, target_recv,
                 block_send, block_recv, sum_send, sum_recv, row_send, row_recv, last_send, last_recv,
                 seg_send, seg_recv, edge_send, edge_recv,
                 seg_send_one, seg_recv_one, edge_send_one, edge_recv_one):
    strip, group = lax.axis_index("seg"), lax.axis_index("sub")
    count = seg * sub
    me = strip * sub + group
    rows = diffusivity.shape[0]
    voxel_rows = noise_ref.shape[0]
    group_voxels = sub * voxel_rows

    def place(peer):
        return peer // sub, lax.rem(peer, sub)

    def rows_of(whose):
        return pl.ds(pl.multiple_of(whose * rows, rows), rows)

    def voxels_of(whose):
        return pl.ds(pl.multiple_of(whose * voxel_rows, voxel_rows), voxel_rows)

    loads = [
        pltpu.make_async_copy(source, target, load_sem.at[index])
        for index, (source, target) in enumerate(
            ((diffusivity_hbm, diffusivity), (flow_hbm, flow), (modes_hbm, modes))
        )
    ]
    for load in loads:
        load.start()
    enter(seg, sub)

    arrive_steps, left_steps = share(
        sub, group, lambda peer: step_ref, lambda whose: steps.at[whose], step_send, step_recv,
        lambda peer: (strip, peer),
    )
    steps[group] = step_ref[...]
    arrive_targets, left_targets = share(
        seg, strip, lambda peer: target_row_ref.at[peer], lambda whose: targets.at[whose],
        target_send, target_recv, lambda peer: (peer, group),
    )
    targets[strip] = target_row_ref[strip]
    loads[0].wait()
    loads[1].wait()
    sems = (seg_send, seg_recv, edge_send, edge_recv)
    copies = start_reshard(seg, sub, [diffusivity[...], flow[...]], packed, edges, strips, edge_in, sems)
    loads[2].wait()
    arrive_steps()
    depth = modes.shape[0] // sub
    turned = steps[...].reshape(sub, LANES).T
    total = None
    for whose in range(sub):
        weight = turned[:depth, whose : whose + 1]
        term = weight * modes[whose * depth : (whose + 1) * depth, :]
        total = term if total is None else total + term
    inlet = jnp.sum(total, axis=0, keepdims=True)
    for t in range(seg):
        own[t + 1] = inlet[:, t * LANES : (t + 1) * LANES]
    right = remote(own.at[seg], sides.at[0], side_send.at[0], side_recv.at[0],
                   strip, lax.rem(group + 1, sub))
    back = remote(own.at[1], sides.at[1], side_send.at[1], side_recv.at[1],
                  strip, lax.rem(group + sub - 1, sub))
    right.start()
    back.start()
    finish_reshard(seg, sub, copies, strips, edge_in, packed, sems)
    right.wait()
    back.wait()
    own[0] = sides[0]
    own[seg + 1] = sides[1]
    lane = lax.broadcasted_iota(jnp.int32, (1, LANES), 1)
    profile[:, :LANES] = own[strip + 1]
    profile[:, LANES:] = jnp.where(lane < HALF, own[strip + 2], own[strip])
    arrive_targets()

    forward_step(strips, profile, field)

    for whose in range(seg):
        voxel = lax.broadcasted_iota(jnp.int32, (group_voxels, rows), 0)
        chosen = jnp.where(voxel == targets[whose], 1.0, 0.0)
        partial[whose * group_voxels : (whose + 1) * group_voxels, :] = choose(
            chosen, field[whose * rows : (whose + 1) * rows, :]
        )
    arrive_sums, left_sums = share(
        count, me, lambda peer: partial.at[voxels_of(peer), :], lambda whose: arrived.at[whose],
        sum_send, sum_recv, place,
    )
    arrived[me] = partial[voxels_of(me), :]
    arrive_blocks, left_blocks = share(
        seg, strip, lambda peer: field.at[rows_of(peer), :], lambda whose: blocks.at[whose],
        block_send, block_recv, lambda peer: (peer, group),
    )
    blocks[strip] = field[rows_of(strip), :]
    arrive_sums()
    voxels = jnp.sum(arrived[...], axis=0)
    spread = spread_ref[...]
    response = lax.dot_general(
        voxels, spread, (((1,), (1,)), ((), ())), precision=HIGH, preferred_element_type=jnp.float32
    )
    response_ref[...] = response
    weighted[...] = jnp.dot(
        noise_ref[...] * response, spread, precision=HIGH, preferred_element_type=jnp.float32
    )
    arrive_rows, left_rows = share(
        sub, group, lambda peer: weighted, lambda whose: gathered.at[voxels_of(whose), :],
        row_send, row_recv, lambda peer: (strip, peer),
    )
    gathered[voxels_of(group), :] = weighted[...]
    arrive_blocks()
    for t in range(seg):
        forward_ref[:, t * LANES : (t + 1) * LANES] = blocks[t]
    arrive_rows()
    everything = gathered[...]
    tiles = []
    for t in range(seg):
        voxel = lax.broadcasted_iota(jnp.int32, (rows, group_voxels), 1)
        chosen = jnp.where(voxel == target_column_ref[:, t : t + 1], 1.0, 0.0)
        tiles.append(choose(chosen, everything))
    sems = (seg_send_one, seg_recv_one, edge_send_one, edge_recv_one)
    copies = start_reshard(seg, sub, [jnp.concatenate(tiles, axis=1)], packed_one, edges_one, driving,
                           edge_in_one, sems)
    finish_reshard(seg, sub, copies, driving, edge_in_one, packed_one, sems)

    adjoint_step(seg, sub, strips, driving, modes, partial_product)

    mine[...] = partial_product[0:1, :]
    arrive_last, left_last = share(
        count, me, lambda peer: mine, lambda whose: products.at[whose], last_send, last_recv, place
    )
    products[me] = mine[...]
    arrive_last()
    product_ref[...] = jnp.sum(products[...], axis=0)
    for left in (left_steps, left_targets, left_sums, left_blocks, left_rows, left_last):
        left()


def on_device(seg, sub, diffusivity, background_flow, inlet_modes, profile_step, brick_owner,
              voxel_row, noise_weight, spread_matrix):
    vmem = pl.BlockSpec(memory_space=pltpu.VMEM)
    anywhere = pl.BlockSpec(memory_space=pl.ANY)
    f32 = jnp.float32
    rows, width = diffusivity.shape
    modes = inlet_modes.shape[0]
    voxel_rows = noise_weight.shape[0]
    total_rows = rows * seg
    count = seg * sub

    def dma(length):
        return [pltpu.SemaphoreType.DMA((length,))] * 2

    def held(*shape, dtype=f32):
        return pltpu.VMEM(shape, dtype)

    step_row = jnp.pad(profile_step[None, :], ((0, 0), (0, LANES - profile_step.shape[0])))
    target = (brick_owner[:, 0] * voxel_rows + voxel_row).reshape(rows, seg)
    forward_field, response, product = pl.pallas_call(
        functools.partial(whole_kernel, seg, sub),
        out_shape=[
            jax.ShapeDtypeStruct((rows, width), f32),
            jax.ShapeDtypeStruct((voxel_rows, LANES), f32),
            jax.ShapeDtypeStruct((1, modes), f32),
        ],
        in_specs=[anywhere] * 3 + [vmem] * 5,
        out_specs=[vmem] * 3,
        scratch_shapes=[
            held(rows, width), held(rows, width), held(modes, width),
            held(2, 2, total_rows, LANES), held(1, 2 * LANES), held(total_rows, LANES),
            held(1, 2, total_rows, LANES), held(CHUNKS, modes),
            held(seg, 2, 2, rows, LANES), held(2, 2, rows, LANES), held(2, total_rows, LANES),
            held(seg, 1, 2, rows, LANES), held(2, 1, rows, LANES), held(1, total_rows, LANES),
            held(sub, 1, LANES), held(seg + 2, 1, LANES), held(2, 1, LANES),
            held(seg, 1, rows, dtype=jnp.int32),
            held(count * voxel_rows, LANES), held(count, voxel_rows, LANES),
            held(voxel_rows, LANES), held(sub * voxel_rows, LANES),
            held(seg, rows, LANES), held(1, modes), held(count, 1, modes),
            pltpu.SemaphoreType.DMA((3,)),
            *dma(sub), *dma(2), *dma(seg), *dma(seg), *dma(count), *dma(sub), *dma(count),
            *dma(seg), pltpu.SemaphoreType.DMA((2,)), pltpu.SemaphoreType.DMA((seg,)),
            *dma(seg), pltpu.SemaphoreType.DMA((2,)), pltpu.SemaphoreType.DMA((seg,)),
        ],
        compiler_params=pltpu.CompilerParams(
            vmem_limit_bytes=VMEM_BYTES, collective_id=0, has_side_effects=True
        ),
    )(diffusivity, background_flow, inlet_modes, step_row, target.T[:, None, :], target, noise_weight,
      spread_matrix)
    share_of = modes // (seg * sub)
    place = lax.axis_index("seg") * sub + lax.axis_index("sub")
    return (forward_field, response, lax.dynamic_slice(product[0], (place * share_of,), (share_of,)))


def solution(mesh):
    return jax.shard_map(
        functools.partial(on_device, mesh.shape["seg"], mesh.shape["sub"]),
        mesh=mesh,
        in_specs=(
            P("seg", "sub"),
            P("seg", "sub"),
            P(None, "sub"),
            P("sub"),
            P(("seg", "sub"), None),
            P(("seg", "sub")),
            P(("seg", "sub"), None),
            P(),
        ),
        out_specs=(P("seg", "sub"), P(("seg", "sub"), None), P(("seg", "sub"))),
        check_vma=False,
    )
```

```python
import functools

import jax
import jax.numpy as jnp
from jax import lax
from jax.experimental import pallas as pl
from jax.experimental.pallas import tpu as pltpu
from jax.sharding import PartitionSpec as P

NV = 2
SC = 2
SIGMA = 0.001
HIGH = lax.Precision.HIGHEST
MESH = pl.DeviceIdType.MESH
LANES = 128
HALF = LANES // 2
CHUNKS = 8
VMEM_BYTES = 60 * 1024 * 1024


def lane_shift(value, amount):
    width = value.shape[-1]
    return pltpu.roll(value, amount % width, axis=value.ndim - 1)


def chunk_shift(value, amount):
    return pltpu.roll(value, amount % value.shape[0], axis=0)


def chunk_index(shape):
    return lax.broadcasted_iota(jnp.int32, shape, 0)


def row_above(value):
    last = value[-1]
    moved = jnp.where(chunk_index(last.shape) > 0, chunk_shift(last, 1), 0.0)
    return jnp.concatenate([moved[None], value[:-1]], axis=0)


def row_below(value):
    first = value[0]
    keep = chunk_index(first.shape) < first.shape[0] - 1
    moved = jnp.where(keep, chunk_shift(first, -1), 0.0)
    return jnp.concatenate([value[1:], moved[None]], axis=0)


def add_columns(value):
    lane = lax.broadcasted_iota(jnp.int32, value.shape, value.ndim - 1)
    partner = jnp.where(lane % 2 == 0, lane_shift(value, -1), lane_shift(value, 1))
    return value + partner


def restrict(value):
    steps = value.shape[0]
    pairs = value.reshape((steps // 2, 2) + value.shape[1:])
    return add_columns(pairs[:, 0] + pairs[:, 1])


def make_plan(diffusion, flow, reaction, stride, forward, inside):
    inverse = 1.0 / (4.0 * diffusion + flow + reaction)
    if forward:
        ahead, gain = diffusion, (diffusion + flow) * inverse
        leftward, rightward = diffusion, diffusion
    else:
        ahead = row_above(diffusion)
        gain = row_below(diffusion + flow) * inverse
        leftward = lane_shift(diffusion, stride) * inside
        rightward = lane_shift(diffusion, -stride) * inside
    steps = gain.shape[0]
    order = range(steps) if forward else range(steps - 1, -1, -1)
    products, running = [None] * steps, None
    for step in order:
        running = gain[step] if running is None else running * gain[step]
        products[step] = running
    count = running.shape[0]
    chunk = chunk_index(running.shape)
    level, jumps, distance = running, [], 1
    while distance < count:
        if forward:
            keep, amount = chunk >= distance, distance
        else:
            keep, amount = chunk < count - distance, -distance
        level = jnp.where(keep, level, 0.0)
        jumps.append(level)
        level = level * chunk_shift(level, amount)
        distance *= 2
    return {
        "inverse": inverse,
        "ahead": ahead,
        "left": leftward,
        "right": rightward,
        "gain": gain,
        "products": jnp.stack(products),
        "jumps": jumps,
        "stride": stride,
        "forward": forward,
    }


def explicit_part(field, plan):
    stride = plan["stride"]
    beside = row_below(field) if plan["forward"] else row_above(field)
    return (
        plan["ahead"] * beside
        + plan["left"] * lane_shift(field, stride)
        + plan["right"] * lane_shift(field, -stride)
    )


def run_rows(driving, plan):
    forward, gain = plan["forward"], plan["gain"]
    steps, count = driving.shape[0], driving.shape[1]
    order = range(steps) if forward else range(steps - 1, -1, -1)
    local, running = [None] * steps, None
    for step in order:
        running = driving[step] if running is None else gain[step] * running + driving[step]
        local[step] = running
    total, distance = running, 1
    for jump in plan["jumps"]:
        total = total + jump * chunk_shift(total, distance if forward else -distance)
        distance *= 2
    chunk = chunk_index(total.shape)
    if forward:
        carry = jnp.where(chunk > 0, chunk_shift(total, 1), 0.0)
    else:
        carry = jnp.where(chunk < count - 1, chunk_shift(total, -1), 0.0)
    return jnp.stack(local) + plan["products"] * carry[None]


def solve(source, finest, coarse):
    field = None
    for cycle_index in range(NV):
        old = None if field is None else explicit_part(field, finest)
        total = source if old is None else source + old
        field = run_rows(total * finest["inverse"], finest)
        new = explicit_part(field, finest)
        coarse_source = restrict(new if old is None else new - old)
        correction = run_rows(coarse_source * coarse["inverse"], coarse)
        for sweep_index in range(1, SC):
            total = coarse_source + explicit_part(correction, coarse)
            correction = run_rows(total * coarse["inverse"], coarse)
        steps = field.shape[0]
        pairs = field.reshape((steps // 2, 2) + field.shape[1:]) + correction[:, None]
        field = pairs.reshape(field.shape)
        total = source + explicit_part(field, finest)
        field = run_rows(total * finest["inverse"], finest)
    return field


def plans(diffusion, flow, forward, inside):
    finest = make_plan(diffusion, flow, SIGMA, 1, forward, inside)
    coarse = make_plan(
        restrict(diffusion) * 0.25, restrict(flow) * 0.5, 4.0 * SIGMA, 2, forward, inside
    )
    return finest, coarse


def take_steps(ref, index):
    rows = ref.shape[-2]
    length = rows // CHUNKS
    halves = [
        jnp.stack([ref[index, half, pl.ds(step, CHUNKS, stride=length), :] for step in range(length)])
        for half in range(2)
    ]
    return jnp.concatenate(halves, axis=2)


def forward_step(strips_ref, profile_ref, field_ref):
    diffusion, flow = take_steps(strips_ref, 0), take_steps(strips_ref, 1)
    finest, coarse = plans(diffusion, flow, True, None)
    first = (diffusion[0] + flow[0]) * profile_ref[...]
    first = jnp.where(chunk_index(first.shape) == 0, first, 0.0)
    source = jnp.concatenate([first[None], jnp.zeros_like(diffusion[1:])], axis=0)
    field = solve(source, finest, coarse)
    length = field.shape[0]
    for step in range(length):
        field_ref[pl.ds(step, CHUNKS, stride=length), :] = field[step, :, :LANES]


def inside_mask(shape, strip, strips, group, groups):
    lane = lax.broadcasted_iota(jnp.int32, shape, len(shape) - 1)
    no_left = jnp.where((strip == 0) & (group == 0), 1, 0)
    no_right = jnp.where((strip == strips - 1) & (group == groups - 1), 1, 0)
    limit_high = jnp.where(no_left == 1, LANES + HALF, 2 * LANES)
    limit_low = jnp.where(no_right == 1, LANES, LANES + HALF)
    outside = (lane >= limit_high) | ((lane >= limit_low) & (lane < LANES + HALF))
    return jnp.where(outside, 0.0, 1.0)


def adjoint_step(seg, sub, strips_ref, driving_ref, modes_ref, partial_ref):
    strip, group = lax.axis_index("seg"), lax.axis_index("sub")
    diffusion, flow = take_steps(strips_ref, 0), take_steps(strips_ref, 1)
    inside = inside_mask((1, 1, 2 * LANES), strip, seg, group, sub)
    finest, coarse = plans(diffusion, flow, False, inside)
    field = solve(take_steps(driving_ref, 0), finest, coarse)
    flux = ((diffusion[0] + flow[0]) * field[0])[:, :LANES]
    flux = jnp.where(chunk_index(flux.shape) == 0, flux, 0.0)
    modes = modes_ref[:, pl.ds(pl.multiple_of(strip * LANES, LANES), LANES)]
    sums = lax.dot_general(
        flux, modes, (((1,), (1,)), ((), ())), precision=HIGH, preferred_element_type=jnp.float32
    )
    partial_ref[...] = sums


def enter(seg, sub):
    strip, group = lax.axis_index("seg"), lax.axis_index("sub")
    barrier = pltpu.get_barrier_semaphore()

    def greet(to_strip, to_group):
        pl.semaphore_signal(barrier, inc=1, device_id=(to_strip, to_group), device_id_type=MESH)

    for k in range(1, seg):
        greet(lax.rem(strip + k, seg), group)
    for k in range(1, sub):
        greet(strip, lax.rem(group + k, sub))

    @pl.when(strip == 0)
    def _():
        for other in range(seg):
            greet(other, lax.rem(group + sub - 1, sub))

    @pl.when(strip == seg - 1)
    def _():
        for other in range(seg):
            greet(other, lax.rem(group + 1, sub))

    pl.semaphore_wait(barrier, seg - 1 + sub - 1 + 2)


def remote(source, target, send, receive, to_strip, to_group):
    return pltpu.make_async_remote_copy(
        src_ref=source,
        dst_ref=target,
        send_sem=send,
        recv_sem=receive,
        device_id=(to_strip, to_group),
        device_id_type=MESH,
    )


def join_halos(one, other):
    lane = lax.broadcasted_iota(jnp.int32, one.shape, 1)
    quarter = HALF // 2
    inner = jnp.where(lane < HALF, lane_shift(other, quarter), lane_shift(other, -quarter))
    return jnp.where((lane < quarter) | (lane >= LANES - quarter), one, inner)


def split_halos(joined):
    lane = lax.broadcasted_iota(jnp.int32, joined.shape, 1)
    quarter = HALF // 2
    other = jnp.where(lane < HALF, lane_shift(joined, -quarter), lane_shift(joined, quarter))
    return joined, other


def join_fields(fields):
    if len(fields) == 2:
        return join_halos(*fields)
    middle = fields[0].shape[0] // 2
    return join_halos(fields[0][:middle], fields[0][middle:])


def start_reshard(seg, sub, fields, packed, edges, inbox, edge_in, sems):
    seg_send, seg_recv, edge_send, edge_recv = sems
    strip, group = lax.axis_index("seg"), lax.axis_index("sub")
    rows = fields[0].shape[0]
    tiles = [[field[:, t * LANES : (t + 1) * LANES] for t in range(seg)] for field in fields]
    lane = lax.broadcasted_iota(jnp.int32, (rows, LANES), 1)
    mains = len(fields) * rows
    for t in range(seg):
        halos = []
        for index, row in enumerate(tiles):
            packed[t, index * rows : (index + 1) * rows, :] = row[t]
            halos.append(jnp.where(lane < HALF, row[min(t + 1, seg - 1)], row[max(t - 1, 0)]))
        packed[t, mains:, :] = join_fields(halos)
    copies = []
    for k in range(1, seg):
        peer = lax.rem(strip + k, seg)
        copies.append(remote(packed.at[peer], inbox.at[strip], seg_send.at[k], seg_recv.at[strip],
                             peer, group))
        copies[-1].start()
    edges[0] = join_fields([row[seg - 1] for row in tiles])
    edges[1] = join_fields([row[0] for row in tiles])
    for side, (to_strip, to_group) in enumerate(((0, group + 1), (seg - 1, group + sub - 1))):
        copies.append(remote(edges.at[side], edge_in.at[strip], edge_send.at[side], edge_recv.at[strip],
                             to_strip, lax.rem(to_group, sub)))
        copies[-1].start()
    inbox[strip] = packed[strip]
    return copies


def finish_reshard(seg, sub, copies, strips, packed, edges, inbox, edge_in, sems):
    seg_send, seg_recv, edge_send, edge_recv = sems
    strip, group = lax.axis_index("seg"), lax.axis_index("sub")
    fields, rows = strips.shape[0], strips.shape[2] // seg
    mains = fields * rows
    for k in range(1, seg):
        peer = lax.rem(strip + k, seg)
        remote(packed.at[peer], inbox.at[peer], seg_send.at[k], seg_recv.at[peer], peer,
               group).wait_recv()

    def take_edges(known, outer):
        for other in range(seg):
            remote(edges.at[0], edge_in.at[other], edge_send.at[0], edge_recv.at[other], 0,
                   group).wait_recv()
            kept = inbox[other, mains:, :]
            lane = lax.broadcasted_iota(jnp.int32, kept.shape, 1)
            use = lane >= HALF if outer else lane < HALF
            inbox[other, mains:, :] = jnp.where(use, edge_in[other] * known, kept)

    @pl.when(strip == 0)
    def _():
        take_edges(jnp.where(group > 0, 1.0, 0.0), True)

    @pl.when(strip == seg - 1)
    def _():
        take_edges(jnp.where(group < sub - 1, 1.0, 0.0), False)

    for other in range(seg):
        start = other * rows
        halos = split_halos(inbox[other, mains:, :])
        for index in range(fields):
            strips[index, 0, start : start + rows, :] = inbox[other, index * rows : (index + 1) * rows, :]
        if fields == 2:
            strips[0, 1, start : start + rows, :] = halos[0]
            strips[1, 1, start : start + rows, :] = halos[1]
        else:
            strips[0, 1, start : start + rows // 2, :] = halos[0]
            strips[0, 1, start + rows // 2 : start + rows, :] = halos[1]


def share(count, me, source_of, target_of, send, recv, place):
    started = []
    for k in range(1, count):
        peer = lax.rem(me + k, count)
        copy = remote(source_of(peer), target_of(me), send.at[k], recv.at[me], *place(peer))
        copy.start()
        started.append(copy)

    def arrive():
        for k in range(1, count):
            peer = lax.rem(me + count - k, count)
            remote(source_of(peer), target_of(peer), send.at[k], recv.at[peer],
                   *place(peer)).wait_recv()

    def left():
        for copy in started:
            copy.wait_send()

    return arrive, left


def choose(chosen, values):
    high = values.astype(jnp.bfloat16)
    rest = values - high.astype(jnp.float32)
    middle = rest.astype(jnp.bfloat16)
    low = (rest - middle.astype(jnp.float32)).astype(jnp.bfloat16)
    picks = chosen.astype(jnp.bfloat16)
    parts = [jnp.dot(picks, part, preferred_element_type=jnp.float32) for part in (low, middle, high)]
    return parts[0] + parts[1] + parts[2]


def whole_kernel(seg, sub, diffusivity_hbm, flow_hbm, modes_hbm, step_ref, owner_ref, voxel_row_ref,
                 noise_ref, spread_ref,
                 forward_ref, response_ref, product_ref,
                 diffusivity, flow, modes, strips, profile, field, driving, partial_product,
                 packed, edges, inbox, edge_in, packed_one, edges_one, inbox_one, edge_in_one,
                 step_row, steps, own, sides, targets, selected,
                 partial, arrived, weighted, gathered, blocks, mine, products, total_row, second,
                 load_sem, step_send, step_recv, side_send, side_recv,
                 block_send, block_recv, sum_send, sum_recv, row_send, row_recv,
                 first_send, first_recv, second_send, second_recv,
                 seg_send, seg_recv, edge_send, edge_recv,
                 seg_send_one, seg_recv_one, edge_send_one, edge_recv_one):
    strip, group = lax.axis_index("seg"), lax.axis_index("sub")
    rows = diffusivity.shape[0]
    voxel_rows = noise_ref.shape[0]
    group_voxels = sub * voxel_rows

    def rows_of(whose):
        return pl.ds(pl.multiple_of(whose * rows, rows), rows)

    def voxels_of(whose):
        return pl.ds(pl.multiple_of(whose * voxel_rows, voxel_rows), voxel_rows)

    loads = [
        pltpu.make_async_copy(source, target, load_sem.at[index])
        for index, (source, target) in enumerate(
            ((diffusivity_hbm, diffusivity), (flow_hbm, flow), (modes_hbm, modes))
        )
    ]
    for load in loads:
        load.start()
    target = owner_ref[...] * voxel_rows + voxel_row_ref[...]
    for part in range(target.shape[0]):
        spread_out = jnp.broadcast_to(target[part : part + 1, :], (LANES, LANES))
        targets[part * LANES : (part + 1) * LANES, :] = spread_out.T
    step_row[...] = jnp.zeros_like(step_row)
    step_row[:, : step_ref.shape[1]] = step_ref[...]
    enter(seg, sub)

    arrive_steps, left_steps = share(
        sub, group, lambda peer: step_row, lambda whose: steps.at[whose], step_send, step_recv,
        lambda peer: (strip, peer),
    )
    steps[group] = step_row[...]
    loads[0].wait()
    loads[1].wait()
    sems = (seg_send, seg_recv, edge_send, edge_recv)
    copies = start_reshard(seg, sub, [diffusivity[...], flow[...]], packed, edges, inbox, edge_in, sems)
    loads[2].wait()
    arrive_steps()
    depth = modes.shape[0] // sub
    turned = steps[...].reshape(sub, LANES).T
    total = None
    for whose in range(sub):
        weight = turned[:depth, whose : whose + 1]
        term = weight * modes[whose * depth : (whose + 1) * depth, :]
        total = term if total is None else total + term
    inlet = jnp.sum(total, axis=0, keepdims=True)
    for t in range(seg):
        own[t + 1] = inlet[:, t * LANES : (t + 1) * LANES]
    right = remote(own.at[seg], sides.at[0], side_send.at[0], side_recv.at[0],
                   strip, lax.rem(group + 1, sub))
    back = remote(own.at[1], sides.at[1], side_send.at[1], side_recv.at[1],
                  strip, lax.rem(group + sub - 1, sub))
    right.start()
    back.start()
    finish_reshard(seg, sub, copies, strips, packed, edges, inbox, edge_in, sems)
    right.wait_recv()
    back.wait_recv()
    sent = copies + [right, back]
    own[0] = sides[0]
    own[seg + 1] = sides[1]
    lane = lax.broadcasted_iota(jnp.int32, (1, LANES), 1)
    profile[:, :LANES] = own[strip + 1]
    profile[:, LANES:] = jnp.where(lane < HALF, own[strip + 2], own[strip])

    forward_step(strips, profile, field)

    arrive, left_blocks = share(
        seg, strip, lambda peer: field.at[rows_of(peer), :], lambda whose: blocks.at[whose],
        block_send, block_recv, lambda peer: (peer, group),
    )
    blocks[strip] = field[rows_of(strip), :]
    voxel = lax.broadcasted_iota(jnp.int32, (rows, LANES), 1)
    picks = []
    for t in range(seg):
        wanted = targets[pl.ds(t, rows, stride=seg), :]
        picks.append(jnp.concatenate(
            [jnp.where(voxel + start == wanted, 1.0, 0.0) for start in range(0, group_voxels, LANES)],
            axis=1,
        ))
    picks_by_voxel = [pick.T for pick in picks]
    arrive()
    partial[...] = choose(
        jnp.concatenate(picks_by_voxel, axis=1), jnp.concatenate([blocks[t] for t in range(seg)], axis=0)
    )
    arrive, left_sums = share(
        sub, group, lambda peer: partial.at[voxels_of(peer), :], lambda whose: arrived.at[whose],
        sum_send, sum_recv, lambda peer: (strip, peer),
    )
    arrived[group] = partial[voxels_of(group), :]
    for t in range(seg):
        forward_ref[:, t * LANES : (t + 1) * LANES] = blocks[t]
    arrive()
    voxels = jnp.sum(arrived[...], axis=0)
    spread = spread_ref[...]
    response = lax.dot_general(
        voxels, spread, (((1,), (1,)), ((), ())), precision=HIGH, preferred_element_type=jnp.float32
    )
    response_ref[...] = response
    weighted[...] = jnp.dot(
        noise_ref[...] * response, spread, precision=HIGH, preferred_element_type=jnp.float32
    )
    arrive_rows, left_rows = share(
        sub, group, lambda peer: weighted, lambda whose: gathered.at[voxels_of(whose), :],
        row_send, row_recv, lambda peer: (strip, peer),
    )
    gathered[voxels_of(group), :] = weighted[...]
    arrive_rows()
    selected[...] = choose(jnp.concatenate(picks, axis=0), gathered[...])
    tiles = [selected[t * rows : (t + 1) * rows, :] for t in range(seg)]
    sems = (seg_send_one, seg_recv_one, edge_send_one, edge_recv_one)
    copies = start_reshard(seg, sub, [jnp.concatenate(tiles, axis=1)], packed_one, edges_one, inbox_one,
                           edge_in_one, sems)
    finish_reshard(seg, sub, copies, driving, packed_one, edges_one, inbox_one, edge_in_one, sems)

    adjoint_step(seg, sub, strips, driving, modes, partial_product)

    mine[...] = partial_product[0:1, :]
    arrive, left_first = share(
        sub, group, lambda peer: mine, lambda whose: products.at[whose], first_send, first_recv,
        lambda peer: (strip, peer),
    )
    products[group] = mine[...]
    arrive()
    total_row[...] = jnp.sum(products[...], axis=0)
    arrive, left_second = share(
        seg, strip, lambda peer: total_row, lambda whose: second.at[whose], second_send, second_recv,
        lambda peer: (peer, group),
    )
    second[strip] = total_row[...]
    arrive()
    product_ref[...] = jnp.sum(second[...], axis=0)
    for left in (left_steps, left_blocks, left_sums, left_rows, left_first, left_second):
        left()
    for copy in sent + copies:
        copy.wait_send()


def on_device(seg, sub, diffusivity, background_flow, inlet_modes, profile_step, brick_owner,
              voxel_row, noise_weight, spread_matrix):
    vmem = pl.BlockSpec(memory_space=pltpu.VMEM)
    anywhere = pl.BlockSpec(memory_space=pltpu.HBM)
    f32 = jnp.float32
    rows, width = diffusivity.shape
    modes = inlet_modes.shape[0]
    voxel_rows = noise_weight.shape[0]
    total_rows = rows * seg

    def dma(length):
        return [pltpu.SemaphoreType.DMA((length,))] * 2

    def held(*shape, dtype=f32):
        return pltpu.VMEM(shape, dtype)

    blocks = brick_owner.shape[0]
    forward_field, response, product = pl.pallas_call(
        functools.partial(whole_kernel, seg, sub),
        out_shape=[
            jax.ShapeDtypeStruct((rows, width), f32),
            jax.ShapeDtypeStruct((voxel_rows, LANES), f32),
            jax.ShapeDtypeStruct((1, modes), f32),
        ],
        in_specs=[anywhere] * 3 + [vmem] * 5,
        out_specs=[vmem] * 3,
        scratch_shapes=[
            held(rows, width), held(rows, width), held(modes, width),
            held(2, 2, total_rows, LANES), held(1, 2 * LANES), held(total_rows, LANES),
            held(1, 2, total_rows, LANES), held(CHUNKS, modes),
            held(seg, 3 * rows, LANES), held(2, rows, LANES),
            held(seg, 3 * rows, LANES), held(seg, rows, LANES),
            held(seg, 3 * rows // 2, LANES), held(2, rows // 2, LANES),
            held(seg, 3 * rows // 2, LANES), held(seg, rows // 2, LANES),
            held(1, LANES), held(sub, 1, LANES), held(seg + 2, 1, LANES), held(2, 1, LANES),
            held(blocks, LANES, dtype=jnp.int32), held(blocks, LANES),
            held(sub * voxel_rows, LANES), held(sub, voxel_rows, LANES),
            held(voxel_rows, LANES), held(sub * voxel_rows, LANES),
            held(seg, rows, LANES), held(1, modes), held(sub, 1, modes), held(1, modes),
            held(seg, 1, modes),
            pltpu.SemaphoreType.DMA((3,)),
            *dma(sub), *dma(2), *dma(seg), *dma(sub), *dma(sub), *dma(sub), *dma(seg),
            *dma(seg), pltpu.SemaphoreType.DMA((2,)), pltpu.SemaphoreType.DMA((seg,)),
            *dma(seg), pltpu.SemaphoreType.DMA((2,)), pltpu.SemaphoreType.DMA((seg,)),
        ],
        compiler_params=pltpu.CompilerParams(
            vmem_limit_bytes=VMEM_BYTES, collective_id=0, has_side_effects=True
        ),
    )(diffusivity, background_flow, inlet_modes, profile_step.reshape(1, -1),
      brick_owner.reshape(-1, LANES), voxel_row.reshape(-1, LANES), noise_weight, spread_matrix)
    share_of = modes // (seg * sub)
    place = lax.axis_index("seg") * sub + lax.axis_index("sub")
    return (forward_field, response, lax.dynamic_slice(product[0], (place * share_of,), (share_of,)))


def solution(mesh):
    return jax.shard_map(
        functools.partial(on_device, mesh.shape["seg"], mesh.shape["sub"]),
        mesh=mesh,
        in_specs=(
            P("seg", "sub"),
            P("seg", "sub"),
            P(None, "sub"),
            P("sub"),
            P(("seg", "sub"), None),
            P(("seg", "sub")),
            P(("seg", "sub"), None),
            P(),
        ),
        out_specs=(P("seg", "sub"), P(("seg", "sub"), None), P(("seg", "sub"))),
        check_vma=False,
    )
```
